32 devices in a mesh: layer: 2 (over y), row: 8 (over z, core), col: 2 (over x).
Axes of the slice: x: 2, y: 2, z: 4, core: 2. Of those that a mesh axis runs over, the one named last changes fastest.
Arguments:
- a_val: float32 [2, 2, 8, 2, 64, 512], P('col', 'layer', 'row'), may hold values from -3 to 3
- a_rows: int32 [2, 2, 8, 2, 8], P('col', 'layer', 'row'), may hold values from 0 to 63, as said below
- b_val: float32 [8, 2, 2, 4, 2, 64, 512], P('row', 'layer', 'col'), may hold values from -3 to 3
- b_cols: int32 [8, 2, 2, 4, 2, 8], P('row', 'layer', 'col'), may hold values from 0 to 63, as said below
- pattern: int32 [2, 8, 256], P('col', 'row'), may hold values from 0 to 4095, as said below
- owners: int32 [2, 2048, 1], P('col', 'row'), may hold values from 0 to 15; in each aligned block of 256 rows (0 to 255, 256 to 511, ..., all dimensions but the last counted through in order) at most 16 rows name the same one
Outputs:
- owned: float32 [2048, 8192], P(('layer', 'row'), 'col')
The draws below stay inside these ranges and needn't reach their ends.
Inputs may be any that keep to these rules, and one draw needn't show every extreme that they name: `a_rows`: for one k, the 8 block rows of A's block column k in a group are distinct and lie in s_k, s_k + 1, ..., s_k + 16 - 1 modulo 64, with s_k the same for every group and for B's block row k. `b_cols`: for one k, the 8 block columns of B's block row k in a group are distinct and lie in s_k, ..., s_k + 16 - 1 modulo 64, with the s_k of A. `pattern`: the 256 entries of one tile are distinct, and for each, (row - column) mod 64 is at most 4 or at least 60. `owners`: at most 16 kept blocks of one tile share an owner, and in every draw some tile has 16 with one owner.
All inputs are finite; a program needn't handle non-finite values.
Results may differ from the reference program's by a relative error of at most 0.0001.
Values sent between devices are 32-bit elements; how exact they have to be, the bound alone decides.
No kernel may reach another device: no remote copies, remote signals or barrier semaphores. Data moves between devices by JAX's collectives and lax.ppermute only.
A program may use at most 64 MiB of HBM per device.

```python
import math
import jax
import jax.numpy as jnp
import numpy as np
from jax import lax

BLOCK = 64
SA = 8
SB = 8
SPREAD = 16
TILE = 64
BAND = 4
KB = 2
NC = 256
CAP = 16
PANEL_SETS = 4
N_LAYER = 2
N_ROW = 8
N_COL = 2


def shared_starts(key):
    return jax.random.randint(jax.random.fold_in(key, 11), (N_LAYER, N_ROW, KB), 0, TILE)


def spread_offsets(key, shape, count):
    scores = jax.random.randint(key, shape + (SPREAD,), 0, 1 << 20) * SPREAD + jnp.arange(SPREAD, dtype=jnp.int32)
    return lax.top_k(scores, count)[1].astype(jnp.int32)


def draw_a_rows(key, part):
    starts = shared_starts(key)
    col_idx = jnp.arange(N_COL, dtype=jnp.int32)[:, None, None, None]
    layer_idx = jnp.arange(N_LAYER, dtype=jnp.int32)[None, :, None, None]
    slot_idx = jnp.arange(N_ROW, dtype=jnp.int32)[None, None, :, None]
    inner_idx = jnp.arange(KB, dtype=jnp.int32)[None, None, None, :]
    label = (slot_idx + col_idx) % N_ROW
    base = starts[layer_idx, label, inner_idx]
    offsets = spread_offsets(jax.random.fold_in(key, 21), (N_COL, N_LAYER, N_ROW, KB), SA)
    return ((base[..., None] + offsets) % TILE).astype(jnp.int32)


def draw_b_cols(key, part):
    starts = shared_starts(key)
    row_idx = jnp.arange(N_ROW, dtype=jnp.int32)[:, None, None, None, None]
    layer_idx = jnp.arange(N_LAYER, dtype=jnp.int32)[None, :, None, None, None]
    col_idx = jnp.arange(N_COL, dtype=jnp.int32)[None, None, :, None, None]
    set_idx = jnp.arange(PANEL_SETS, dtype=jnp.int32)[None, None, None, :, None]
    inner_idx = jnp.arange(KB, dtype=jnp.int32)[None, None, None, None, :]
    label = (row_idx + col_idx + set_idx * N_COL) % N_ROW
    base = starts[layer_idx, label, inner_idx]
    offsets = spread_offsets(jax.random.fold_in(key, 22), (N_ROW, N_LAYER, N_COL, PANEL_SETS, KB), SB)
    return ((base[..., None] + offsets) % TILE).astype(jnp.int32)


def draw_pattern(key, part):
    rows = jnp.arange(TILE, dtype=jnp.int32)[:, None]
    cols = jnp.arange(TILE, dtype=jnp.int32)[None, :]
    diagonal = (rows - cols) % TILE
    inband = ((diagonal <= BAND) | (diagonal >= TILE - BAND)).astype(jnp.int32).reshape(-1)
    code = (rows * TILE + cols).reshape(-1)
    noise = jax.random.randint(jax.random.fold_in(key, 31), (N_COL, N_ROW, TILE * TILE), 0, 4096)
    score = inband * (1 << 24) + noise * (TILE * TILE) + code
    return lax.top_k(score, NC)[1].astype(jnp.int32)


def level_of(key, extent, split, smallest, high):
    factor_of = 1.0
    for axis_at, parts in split:
        draws = jax.random.uniform(jax.random.fold_in(jax.random.fold_in(key, 6), axis_at), (parts,), jnp.float32, smallest / len(split), high / len(split))
        factor_of = factor_of * jnp.repeat(jnp.exp(draws), extent[axis_at] // parts).reshape((-1,) + (1,) * (len(extent) - 1 - axis_at))
    return factor_of


def deal_out(rng, own, number, rows, number_of, top, reach, lean):
    ranking = jax.random.permutation(rng, number_of)
    crowded, usual = portions_of(number_of, rows * top, reach, lean, True), portions_of(number_of, rows * top, reach, lean, False)
    places = jnp.arange(number_of)

    def named(sizes, turn):
        used = int((sizes > 0).sum())
        fixed = max(1, used // 4)
        moved = fixed + (places - fixed + turn * (used - fixed)) % max(1, number_of - fixed)
        return jnp.zeros((number_of,), jnp.int32).at[ranking[jnp.where(places < fixed, places, moved)]].set(jnp.asarray(sizes, jnp.int32))

    sizes = jnp.where(number % 4 == 0, named(crowded, number // 4), named(usual, number - number // 4 - 1))
    mixed = jax.random.permutation(jax.random.fold_in(own, 3), number_of)
    source_of, taker = mixed[0:number_of // 2 * 2:2], mixed[1:number_of // 2 * 2:2]
    slack = jnp.minimum(sizes[source_of] - 1, reach - sizes[taker]) // 2
    slack = jnp.where((source_of == ranking[0]) | (taker == ranking[0]) | (sizes[taker] == 0), 0, jnp.maximum(slack, 0))
    moved = jax.random.randint(jax.random.fold_in(own, 4), (number_of // 2,), 0, 1 << 20) % (slack + 1)
    sizes = sizes.at[source_of].add(-moved).at[taker].add(moved)
    items = jnp.searchsorted(jnp.cumsum(sizes), jnp.arange(rows * top), side="right").astype(jnp.int32)
    listing = items.reshape(top, rows).T
    listing = listing[jax.random.permutation(jax.random.fold_in(own, 1), rows)]
    turn = jax.random.randint(jax.random.fold_in(own, 2), (rows, 1), 0, top)
    return jnp.take_along_axis(listing, (jnp.arange(top)[None, :] + turn) % top, axis=1)


def portions_of(amount, total, limit, slope, full):
    loads = [(1 << 20) // math.isqrt(grade ** slope) + 1 for grade in range(1, amount + 1)]
    largest = limit if full else min(limit, max(-(-total // amount), total * loads[0] // sum(loads)))
    least = 1 if total - largest >= amount - 1 else 0
    given, rest = [largest] + [least] * (amount - 1), total - largest - least * (amount - 1)
    while rest > 0:
        free = [i for i in range(1, amount) if given[i] < largest] or [i for i in range(1, amount) if given[i] < limit]
        mass, remaining = sum([loads[i] for i in free]), rest
        for i in free:
            more = min(limit - given[i], max(1, remaining * loads[i] // mass), rest)
            given[i] = given[i] + more
            rest = rest - more
    return np.array(given)


def scatter_about(stream_key, extent, deviation, limit, shards=(), kind=jnp.bfloat16):
    drawn = deviation * jax.random.normal(stream_key, extent, jnp.float32)
    if shards:
        drawn = drawn * level_of(stream_key, extent, shards, -0.22, 0.18)
    return jnp.clip(drawn, -limit, limit).astype(kind)


def setup_inputs(seed: int = 0) -> dict:
    arg_keys = jax.random.split(jax.random.key(seed), 7)
    a_val = scatter_about(arg_keys[0], (N_COL, N_LAYER, N_ROW, KB, BLOCK, SA * BLOCK), 0.2, 3.0, ((0, 2), (1, 2), (2, 8)), jnp.float32)
    a_rows = draw_a_rows(jax.random.fold_in(arg_keys[6], 71), 0)
    b_val = scatter_about(arg_keys[2], (N_ROW, N_LAYER, N_COL, PANEL_SETS, KB, BLOCK, SB * BLOCK), 0.2, 3.0, ((0, 8), (1, 2), (2, 2)), jnp.float32)
    b_cols = draw_b_cols(jax.random.fold_in(arg_keys[6], 71), 0)
    pattern = draw_pattern(jax.random.fold_in(arg_keys[6], 71), 0)
    owners_keys = jax.random.split(jax.random.fold_in(arg_keys[5], 1), N_COL * (N_ROW * NC) // NC)
    owners_turns = jax.random.permutation(jax.random.fold_in(arg_keys[5], 3), N_COL * (N_ROW * NC) // NC)
    owners = jax.vmap(lambda own, number: deal_out(jax.random.fold_in(arg_keys[5], 2), own, number, NC, N_LAYER * N_ROW, 1, CAP, 2))(owners_keys, owners_turns).reshape((N_COL, N_ROW * NC, 1))
    return {"a_val": a_val, "a_rows": a_rows, "b_val": b_val, "b_cols": b_cols, "pattern": pattern, "owners": owners}


def products(a_panel, a_index, b_panel, b_index, table):
    count = a_panel.shape[0]
    prod = jnp.einsum("kxp,kxq->kpq", a_panel, b_panel, precision=lax.Precision.HIGHEST, preferred_element_type=jnp.float32)
    prod = prod.reshape(count, SA, BLOCK, SB, BLOCK).transpose(0, 1, 3, 2, 4).reshape(count * SA * SB, BLOCK * BLOCK)
    target = table[(a_index[:, :, None] * TILE + b_index[:, None, :]).reshape(-1)]
    return prod, target


def reference(a_val, a_rows, b_val, b_cols, pattern, owners):
    n_owner = N_LAYER * N_ROW
    span = BLOCK * BLOCK

    def tile_total(index, owned):
        row_group = index // N_COL
        col_group = index % N_COL
        kept_list = pattern[col_group, row_group]
        table = jnp.full((TILE * TILE,), NC, jnp.int32).at[kept_list].set(jnp.arange(NC, dtype=jnp.int32))

        def panel(step, total):
            layer = step // N_ROW
            label = step % N_ROW
            source_a = (label - col_group) % N_ROW
            offset = (label - row_group) % N_ROW
            source_b = offset % N_COL
            set_index = offset // N_COL
            prod, target = products(a_val[col_group, layer, source_a], a_rows[col_group, layer, source_a],
                                    b_val[row_group, layer, source_b, set_index], b_cols[row_group, layer, source_b, set_index], table)
            return total.at[target].add(prod)

        total = lax.fori_loop(0, N_LAYER * N_ROW, panel, jnp.zeros((NC + 1, span), jnp.float32))
        owner_list = lax.dynamic_slice_in_dim(owners[col_group, :, 0], (row_group * NC).astype(jnp.int32), NC)
        onehot = (owner_list[:, None] == jnp.arange(n_owner, dtype=jnp.int32)[None, :]).astype(jnp.int32)
        rank = jnp.sum((jnp.cumsum(onehot, axis=0) - onehot) * onehot, axis=1)
        places = (owner_list * N_ROW + row_group) * CAP + rank
        return owned.at[places, col_group].set(total[:NC])

    owned = lax.fori_loop(0, N_ROW * N_COL, tile_total, jnp.zeros((n_owner * N_ROW * CAP, N_COL, span), jnp.float32))
    return owned.reshape(n_owner * N_ROW * CAP, N_COL * span)
```

```python
import functools
import jax
import jax.numpy as jnp
from jax import lax
from jax.experimental import pallas as pl
from jax.experimental.pallas import tpu as pltpu
from jax.sharding import PartitionSpec as P

TILE = 64
CAP = 16
LANES = 128
VMEM_BYTES = 56 * 2**20


def swap(block, axis, mask):
    return lax.ppermute(block, axis, [(i, i ^ mask) for i in range(lax.axis_size(axis))])


def gathered(block, axis, order):
    held = {0: block}
    for mask in order:
        held[mask] = jax.tree.map(
            lambda x, low=mask & -mask: swap(x, axis, low), held[mask & (mask - 1)]
        )
    return [held[mask] for mask in range(lax.axis_size(axis))]


def pack_kernel(a_ref, rows_ref, out_ref, flipped):
    panels, block, width = a_ref.shape
    half = width // 2
    for kk in range(panels):
        flipped[...] = a_ref[kk].T
        out_ref[pl.ds(kk * half, half), :block] = flipped[pl.ds(0, half, 2), :]
        out_ref[pl.ds(kk * half, half), block:] = flipped[pl.ds(1, half, 2), :]
    tail = panels * half
    out_ref[pl.ds(tail, 8), :] = jnp.zeros((8, LANES), jnp.float32)
    out_ref[pl.ds(tail, panels), : rows_ref.shape[1]] = rows_ref[...].astype(jnp.float32)


def product_kernel(n_layer, n_row, n_col, panels, sets, many, table_ref, *refs):
    a_refs, refs = refs[:n_row], refs[n_row:]
    b_refs, refs = refs[:n_col], refs[n_col:]
    c_refs, refs = refs[:n_col], refs[n_col:]
    n_unit = n_layer * n_row
    out_refs, refs = refs[:n_unit], refs[n_unit:]
    acc, left, right, prod, index, number, sem = refs
    block = b_refs[0].shape[1]
    half = many * block // 2
    pair = block // 2
    low = lax.broadcasted_iota(jnp.int32, (1, LANES), 1) < block

    for m in range(n_row):
        tail = a_refs[m][pl.ds(panels * half, panels), :]
        index[pl.ds(m * panels, panels), :] = tail.astype(jnp.int32)
    for m in range(n_col):
        index[pl.ds(n_row * panels + m, 1), : c_refs[m].shape[1]] = c_refs[m][...]
    copy = pltpu.make_async_copy(index, number, sem)
    copy.start()

    @pl.loop(0, acc.shape[0] // (8 * pair))
    def _(i):
        acc[pl.ds(pl.multiple_of(i * 8 * pair, 8), 8 * pair), :] = jnp.zeros(
            (8 * pair, LANES), jnp.float32
        )

    for m in range(n_col):

        @pl.loop(0, sets * panels)
        def _(i, m=m):
            b = b_refs[m][i]
            high = b.astype(jnp.bfloat16)
            rest = (b - high.astype(jnp.float32)).astype(jnp.bfloat16)
            at = m * sets * panels + i
            right[at, pl.ds(0, block), :] = high
            right[at, pl.ds(block, block), :] = rest
            right[at, pl.ds(2 * block, block), :] = high
            right[at, pl.ds(3 * block, block), :] = jnp.zeros_like(high)

    for m in range(n_row):

        @pl.loop(0, panels)
        def _(kk, m=m):
            a = a_refs[m][pl.ds(pl.multiple_of(kk * half, half), half), :]
            turned = pltpu.roll(a, block, 1)
            rest = a - a.astype(jnp.bfloat16).astype(jnp.float32)
            turned_rest = pltpu.roll(rest, block, 1)
            at = m * panels + kk
            left[at, pl.ds(0, half), pl.ds(0, LANES)] = jnp.where(low, a, turned).astype(jnp.bfloat16)
            left[at, pl.ds(0, half), pl.ds(LANES, LANES)] = rest.astype(jnp.bfloat16)
            left[at, pl.ds(half, half), pl.ds(0, LANES)] = jnp.where(low, turned, a).astype(jnp.bfloat16)
            left[at, pl.ds(half, half), pl.ds(LANES, LANES)] = turned_rest.astype(jnp.bfloat16)

    copy.wait()
    my_row, my_col = lax.axis_index("row"), lax.axis_index("col")

    def place_b(m):
        label = lax.rem(lax.bitwise_xor(my_row, m) + my_col, n_row)
        offset = lax.rem(label - my_row + n_row, n_row)
        mask = lax.bitwise_xor(lax.rem(offset, n_col), my_col)
        return mask, lax.div(offset, n_col)

    def multiply(m, kk):
        mask, which = place_b(m)
        prod[kk] = jnp.dot(
            left[m * panels + kk],
            right[(mask * sets + which) * panels + kk],
            preferred_element_type=jnp.float32,
        )

    def add(m, kk):
        mask, which = place_b(m)
        base = (which * panels + kk) * many
        cols = [number[n_row * panels + mask, base + b] for b in range(many)]
        for a in range(many):
            row = number[m * panels + kk, a]
            first, second = lax.shift_right_logical(row, 1), lax.bitwise_and(row, 1) * TILE
            places = [pl.multiple_of(table_ref[first, second + col], pair) for col in cols]
            even = prod[kk, pl.ds(a * pair, pair), :]
            odd = prod[kk, pl.ds(half + a * pair, pair), :]
            blocks = []
            for q in range(many // 2):
                e, o = even[:, q * LANES : (q + 1) * LANES], odd[:, q * LANES : (q + 1) * LANES]
                turned = pltpu.roll(jnp.where(low, o, e), block, 1)
                blocks += [jnp.where(low, e, turned), jnp.where(low, turned, o)]
            sums = [acc[pl.ds(at, pair), :] + new for at, new in zip(places, blocks)]
            for at, new in zip(places, sums):
                acc[pl.ds(at, pair), :] = new

    multiply(0, 0)

    @pl.loop(0, n_row)
    def _(m):
        for kk in range(panels):
            if kk + 1 < panels:
                multiply(m, kk + 1)
            else:
                multiply(lax.rem(m + 1, n_row), 0)
            add(m, kk)

    @pl.loop(0, pair)
    def _(j):
        for unit in range(n_unit):
            for eight in range(CAP // 8):
                first = (unit * CAP + eight * 8) * pair
                out_refs[unit][eight, j] = acc[pl.ds(first + j, 8, pair), :]


def place_kernel(n_row, own_ref, other_ref, *refs):
    units, out_ref, total, sems = refs[: n_row - 1], refs[n_row - 1], refs[n_row], refs[n_row + 1]
    my_row = lax.axis_index("row")
    size = own_ref.shape[0]

    def copy(m, source):
        at = pl.multiple_of(lax.bitwise_xor(my_row, m) * size, size)
        return pltpu.make_async_copy(source, out_ref.at[pl.ds(at, size)], sems.at[m])

    copies = [copy(m, units[m - 1]) for m in range(1, n_row)]
    for c in copies:
        c.start()
    total[...] = own_ref[...] + other_ref[...]
    mine = copy(0, total)
    mine.start()
    for c in (*copies, mine):
        c.wait()


def far_first(n):
    return [m for m in range(n // 2, n)] + [m for m in range(2, n // 2)] + [1, 0]


def body(a_val, a_rows, b_val, b_cols, pattern, owners):
    n_row, n_col, n_layer = (lax.axis_size(x) for x in ("row", "col", "layer"))
    panels, block, width = a_val.shape[3:]
    sets = b_val.shape[3]
    many = width // block
    pair = block // 2
    kept = pattern.shape[2]
    a_val, a_rows = a_val[0, 0, 0], a_rows[0, 0, 0]
    b_val = b_val[0, 0, 0].reshape(sets * panels, block, width)
    b_cols = b_cols[0, 0, 0].reshape(1, sets * panels * many)
    vmem, anywhere = pl.BlockSpec(memory_space=pltpu.VMEM), pl.BlockSpec(memory_space=pl.ANY)
    params = pltpu.CompilerParams(vmem_limit_bytes=VMEM_BYTES)
    rows = panels * width // 2 + 8

    packed = pl.pallas_call(
        pack_kernel,
        out_shape=jax.ShapeDtypeStruct((rows, LANES), jnp.float32),
        in_specs=[vmem, vmem],
        out_specs=vmem,
        scratch_shapes=[pltpu.VMEM((width, block), jnp.float32)],
        compiler_params=params,
    )(a_val, a_rows)
    b_held = gathered((b_val, b_cols), "col", range(1, n_col))
    high_first = [m for m in range(1, n_row)]
    high_first.sort(key=lambda m: (m & 1, bin(m).count("1"), -m))
    a_held = gathered(packed, "row", high_first)

    owner = owners[0, :, 0]
    my_row, my_layer = lax.axis_index("row"), lax.axis_index("layer")
    before = (owner[:, None] == owner[None, :]) & (
        jnp.arange(kept)[None, :] < jnp.arange(kept)[:, None]
    )
    rank = jnp.sum(before.astype(jnp.int32), axis=1)
    unit = ((owner // n_row) ^ my_layer) * n_row + ((owner % n_row) ^ my_row)
    slots = n_layer * n_row * CAP
    slot = unit * CAP + rank
    codes = jnp.arange(TILE * TILE, dtype=jnp.int32)
    hit = codes[:, None] == pattern[0, 0][None, :]
    table = slots + jnp.sum(jnp.where(hit, slot[None, :] - slots, 0), axis=1)
    table = (table * pair).reshape(TILE * TILE // LANES, LANES)

    unit_shape = (CAP // 8, pair, 8, LANES)
    n_unit = n_layer * n_row
    index_rows = -(-(n_row * panels + n_col) // 8) * 8
    parts = pl.pallas_call(
        functools.partial(product_kernel, n_layer, n_row, n_col, panels, sets, many),
        out_shape=[jax.ShapeDtypeStruct(unit_shape, jnp.float32)] * n_unit,
        in_specs=[pl.BlockSpec(memory_space=pltpu.SMEM)] + [vmem] * (n_row + 2 * n_col),
        out_specs=[vmem] * n_unit,
        scratch_shapes=[
            pltpu.VMEM(((slots + 8) * pair, LANES), jnp.float32),
            pltpu.VMEM((n_row * panels, width, 4 * block), jnp.bfloat16),
            pltpu.VMEM((n_col * sets * panels, 4 * block, width), jnp.bfloat16),
            pltpu.VMEM((panels, width, width), jnp.float32),
            pltpu.VMEM((index_rows, LANES), jnp.int32),
            pltpu.SMEM((index_rows, LANES), jnp.int32),
            pltpu.SemaphoreType.DMA,
        ],
        compiler_params=params,
    )(table, *a_held, *[b[0] for b in b_held], *[b[1] for b in b_held])

    arrived, others = {}, []
    order = far_first(n_row)
    for at, m in enumerate(order):
        gone = parts[n_row + m]
        if at > 1:
            gone, others[at - 2] = lax.optimization_barrier((gone, others[at - 2]))
        if at > 3 and order[at - 4] in arrived and at < n_row - 1:
            gone, arrived[order[at - 4]] = lax.optimization_barrier((gone, arrived[order[at - 4]]))
        other = swap(gone, "layer", 1)
        others.append(other)
        if m:
            arrived[m] = swap(parts[m] + other, "row", m)
    owned = pl.pallas_call(
        functools.partial(place_kernel, n_row),
        out_shape=jax.ShapeDtypeStruct((n_row * unit_shape[0], *unit_shape[1:]), jnp.float32),
        in_specs=[vmem] * (n_row + 1),
        out_specs=anywhere,
        scratch_shapes=[
            pltpu.VMEM(unit_shape, jnp.float32),
            pltpu.SemaphoreType.DMA((n_row,)),
        ],
        compiler_params=params,
    )(parts[0], other, *[arrived[m] for m in range(1, n_row)])
    return owned.transpose(0, 2, 1, 3).reshape(n_row * CAP, block * block)


def solution(mesh):
    return jax.shard_map(
        body,
        mesh=mesh,
        in_specs=(
            P("col", "layer", "row", None, None, None),
            P("col", "layer", "row", None, None),
            P("row", "layer", "col", None, None, None, None),
            P("row", "layer", "col", None, None, None),
            P("col", "row", None),
            P("col", "row", None),
        ),
        out_specs=P(("layer", "row"), "col"),
        check_vma=False,
    )
```

```python
import functools
import jax
import jax.numpy as jnp
from jax import lax
from jax.experimental import pallas as pl
from jax.experimental.pallas import tpu as pltpu
from jax.sharding import PartitionSpec as P

TILE = 64
CAP = 16
LANES = 128
MIB = 2**20
LAG_Y = 4
LAG_Z = 5


def swap(block, axis, mask):
    return lax.ppermute(block, axis, [(i, i ^ mask) for i in range(lax.axis_size(axis))])


def gathered(block, axis, order):
    held = {0: block}
    for mask in order:
        held[mask] = jax.tree.map(
            lambda x, low=mask & -mask: swap(x, axis, low), held[mask & (mask - 1)]
        )
    return [held[mask] for mask in range(lax.axis_size(axis))]


def gathered_with(block, axis, order, early):
    held = {0: block}
    for mask in order:
        source = held[mask & (mask - 1)]
        if mask == 3:
            source, early = lax.optimization_barrier((source, early))
            held[mask & (mask - 1)], done = source, early
        held[mask] = swap(source, axis, mask & -mask)
    return [held[mask] for mask in range(lax.axis_size(axis))], done


def parts_of(pair):
    return ((0, pair),)


def pack_a_kernel(a_ref, rows_ref, out_ref, flipped):
    panels, block, width = a_ref.shape
    half, pair, many = width // 2, block // 2, width // block
    for kk in range(panels):
        flipped[...] = a_ref[kk].T
        for first, last in parts_of(pair):
            long = last - first
            for a in range(many):
                at = kk * half + many * first + a * long
                for odd in range(2):
                    taken = flipped[pl.ds(a * block + 2 * first + odd, long, 2), :]
                    out_ref[pl.ds(at, long), odd * block : (odd + 1) * block] = taken
    out_ref[pl.ds(panels * half, 8), :] = jnp.zeros((8, LANES), jnp.float32)
    out_ref[pl.ds(panels * half, panels), :many] = rows_ref[...].astype(jnp.float32)


def pack_b_kernel(b_ref, cols_ref, out_ref):
    count, block, width = b_ref.shape

    @pl.loop(0, count)
    def _(i):
        out_ref[pl.ds(pl.multiple_of(i * block, block), block), :] = b_ref[i]

    out_ref[pl.ds(count * block, 8), :] = jnp.zeros((8, width), jnp.float32)
    out_ref[pl.ds(count * block, count), : cols_ref.shape[1]] = cols_ref[...].astype(jnp.float32)


def product_kernel(n_row, n_col, panels, sets, first, groups, table_ref, *refs):
    a_refs, refs = refs[:n_row], refs[n_row:]
    b_refs, refs = refs[:n_col], refs[n_col:]
    n_out = len(refs) - 8
    out_refs, refs = refs[:n_out], refs[n_out:]
    acc, left, right, prod, index, target, number, sem = refs
    block, width = right.shape[1] // 4, right.shape[2]
    many = width // block
    half = width // 2
    long = left.shape[1] // (2 * many)
    rows = many * long
    low = lax.broadcasted_iota(jnp.int32, (1, LANES), 1) < block

    my_row, my_col = lax.axis_index("row"), lax.axis_index("col")

    def place_b(m):
        label = lax.rem(lax.bitwise_xor(my_row, m) + my_col, n_row)
        offset = lax.rem(label - my_row + n_row, n_row)
        mask = lax.bitwise_xor(lax.rem(offset, n_col), my_col)
        return mask, lax.div(offset, n_col)

    count = n_row * panels
    for m in range(n_row):
        index[pl.ds(m * panels, panels), :] = a_refs[m][pl.ds(panels * half, panels), :]
    for m in range(n_col):
        tail = b_refs[m][pl.ds(sets * panels * block, sets * panels), pl.ds(0, LANES)]
        index[pl.ds(count + m * sets * panels, sets * panels), :] = tail
    down = index[pl.ds(0, count), :].T.astype(jnp.int32)
    across = lax.broadcasted_iota(jnp.int32, (many, LANES), 1)
    hot = [jnp.where(down[:many, k : k + 1] == across, 1.0, 0.0) for k in range(count)]
    hot = jnp.concatenate(hot, axis=0)[:, :TILE].astype(jnp.bfloat16)
    entries = table_ref[...]
    halves = [lax.shift_right_logical(entries, 4), lax.bitwise_and(entries, 15)]
    upper, lower = [
        jnp.dot(hot, x.astype(jnp.float32).astype(jnp.bfloat16), preferred_element_type=jnp.float32) for x in halves
    ]
    found = (upper * 16 + lower).astype(jnp.int32) * long
    per_row = LANES // many
    for k in range(count):
        mask, which = place_b(k // panels)
        at = count + (mask * sets + which) * panels + k % panels
        cols = jnp.broadcast_to(index[pl.ds(at, 1), :], (many, LANES)).astype(jnp.int32)
        picked = jnp.take_along_axis(found[k * many : (k + 1) * many, :], cols, axis=1)
        picked = jnp.where(across < many, picked, 0)
        shift = k % per_row * many
        picked = pltpu.roll(picked, shift, 1) if shift else picked
        group = pl.ds(k // per_row * many, many)
        target[group, :] = picked if shift == 0 else target[group, :] + picked
    copy = pltpu.make_async_copy(target, number, sem)
    copy.start()

    @pl.loop(0, acc.shape[0] // (8 * long))
    def _(i):
        acc[pl.ds(pl.multiple_of(i * 8 * long, 8), 8 * long), :] = jnp.zeros((8 * long, LANES), jnp.float32)

    for m in range(n_row):

        @pl.loop(0, panels)
        def _(kk, m=m):
            a = a_refs[m][pl.ds(pl.multiple_of(kk * half + many * first, 8), rows), :]
            turned = pltpu.roll(a, block, 1)
            rest = a - a.astype(jnp.bfloat16).astype(jnp.float32)
            turned_rest = pltpu.roll(rest, block, 1)
            at = m * panels + kk
            left[at, pl.ds(0, rows), pl.ds(0, LANES)] = jnp.where(low, a, turned).astype(jnp.bfloat16)
            left[at, pl.ds(0, rows), pl.ds(LANES, LANES)] = rest.astype(jnp.bfloat16)
            left[at, pl.ds(rows, rows), pl.ds(0, LANES)] = jnp.where(low, turned, a).astype(jnp.bfloat16)
            left[at, pl.ds(rows, rows), pl.ds(LANES, LANES)] = turned_rest.astype(jnp.bfloat16)

    for m in range(n_col):

        @pl.loop(0, sets * panels)
        def _(i, m=m):
            b = b_refs[m][pl.ds(pl.multiple_of(i * block, block), block), :]
            high = b.astype(jnp.bfloat16)
            rest = (b - high.astype(jnp.float32)).astype(jnp.bfloat16)
            at = m * sets * panels + i
            right[at, pl.ds(0, block), :] = high
            right[at, pl.ds(block, block), :] = rest
            right[at, pl.ds(2 * block, block), :] = high
            right[at, pl.ds(3 * block, block), :] = jnp.zeros_like(high)

    copy.wait()

    def multiply(m, kk):
        mask, which = place_b(m)
        prod[kk] = jnp.dot(
            left[m * panels + kk],
            right[(mask * sets + which) * panels + kk],
            preferred_element_type=jnp.float32,
        )

    def add(m, kk):
        k = m * panels + kk
        group, start = lax.div(k, per_row) * many, lax.rem(k, per_row) * many
        for a in range(many):
            places = [pl.multiple_of(number[group + a, start + b], 8) for b in range(many)]
            even = prod[kk, pl.ds(a * long, long), :]
            odd = prod[kk, pl.ds(rows + a * long, long), :]
            blocks = []
            for q in range(many // 2):
                e, o = even[:, q * LANES : (q + 1) * LANES], odd[:, q * LANES : (q + 1) * LANES]
                turned = pltpu.roll(jnp.where(low, o, e), block, 1)
                blocks += [jnp.where(low, e, turned), jnp.where(low, turned, o)]
            sums = [acc[pl.ds(at, long), :] + new for at, new in zip(places, blocks)]
            for at, new in zip(places, sums):
                acc[pl.ds(at, long), :] = new

    multiply(0, 0)

    @pl.loop(0, n_row)
    def _(m):
        for kk in range(panels):
            if kk + 1 < panels:
                multiply(m, kk + 1)
            else:
                multiply(lax.rem(m + 1, n_row), 0)
            add(m, kk)

    @pl.loop(0, long // 8)
    def _(j):
        at = pl.multiple_of(j * 8, 8)
        for out, out_ref in enumerate(out_refs):
            layer, group = divmod(out, len(groups))
            for i, m in enumerate(groups[group]):
                for eight in range(CAP // 8):
                    start = ((layer * n_row + m) * CAP + eight * 8) * long
                    taken = [acc[pl.ds(pl.multiple_of(start + s * long + at, 8), 8), :] for s in range(8)]
                    out_ref[i, eight, pl.ds(at, 8)] = jnp.swapaxes(jnp.stack(taken), 0, 1)


def place_kernel(pieces, *refs):
    sources, out_ref, sems = refs[: len(pieces)], refs[len(pieces)], refs[len(pieces) + 1]
    my_row = lax.axis_index("row")
    copies = []
    for i, (m, first) in enumerate(pieces):
        size, long = sources[i].shape[:2]
        at = pl.multiple_of(lax.bitwise_xor(my_row, m) * size, size)
        target = out_ref.at[pl.ds(at, size), pl.ds(first, long)]
        copies.append(pltpu.make_async_copy(sources[i], target, sems.at[i]))
    for copy in copies:
        copy.start()
    for copy in copies:
        copy.wait()


def body(a_val, a_rows, b_val, b_cols, pattern, owners):
    n_row, n_col, n_layer = (lax.axis_size(x) for x in ("row", "col", "layer"))
    panels, block, width = a_val.shape[3:]
    sets = b_val.shape[3]
    many = width // block
    pair = block // 2
    kept = pattern.shape[2]
    a_val, a_rows = a_val[0, 0, 0], a_rows[0, 0, 0]
    b_val = b_val[0, 0, 0].reshape(sets * panels, block, width)
    b_cols = b_cols[0, 0, 0].reshape(sets * panels, many)
    vmem, anywhere = pl.BlockSpec(memory_space=pltpu.VMEM), pl.BlockSpec(memory_space=pl.ANY)

    def room(*arrays):
        return pltpu.CompilerParams(vmem_limit_bytes=2 * MIB + sum(arrays))

    a_shape = (panels * width // 2 + 8, LANES)
    b_shape = (sets * panels * block + 8, width)

    a_packed = pl.pallas_call(
        pack_a_kernel,
        out_shape=jax.ShapeDtypeStruct(a_shape, jnp.float32),
        in_specs=[vmem] * 2,
        out_specs=vmem,
        scratch_shapes=[pltpu.VMEM((width, block), jnp.float32)],
        compiler_params=room(a_val.size * 8, width * LANES * 4),
    )(a_val, a_rows)
    b_packed = pl.pallas_call(
        pack_b_kernel,
        out_shape=jax.ShapeDtypeStruct(b_shape, jnp.float32),
        in_specs=[vmem] * 2,
        out_specs=vmem,
        compiler_params=room(b_val.size * 8),
    )(b_val, b_cols)
    b_held = gathered(b_packed, "col", range(1, n_col))

    owner = owners[0, :, 0]
    my_row, my_layer = lax.axis_index("row"), lax.axis_index("layer")
    before = (owner[:, None] == owner[None, :]) & (
        jnp.arange(kept)[None, :] < jnp.arange(kept)[:, None]
    )
    rank = jnp.sum(before.astype(jnp.int32), axis=1)
    unit = ((owner // n_row) ^ my_layer) * n_row + ((owner % n_row) ^ my_row)
    slots = n_layer * n_row * CAP
    slot = unit * CAP + rank
    codes = jnp.arange(TILE * TILE, dtype=jnp.int32)
    hit = codes[:, None] == pattern[0, 0][None, :]
    table = slots + jnp.sum(jnp.where(hit, slot[None, :] - slots, 0), axis=1)
    table = jnp.pad(table.reshape(TILE, TILE), ((0, 0), (0, LANES - TILE)))

    high_first = sorted(range(1, n_row), key=lambda m: (m & 1, m.bit_count(), -m))
    a_held, table = gathered_with(a_packed, "row", high_first, table)

    b_count = n_col * sets * panels
    held_bytes = n_row * a_shape[0] * LANES * 4 + n_col * b_shape[0] * width * 4
    far, near = list(range(n_row // 2, n_row)), [*range(2, n_row // 2), 1, 0]

    def products(first, last, groups, table):
        long = last - first
        shapes = [(len(g), CAP // 8, long, 8, LANES) for g in groups] * n_layer
        scratch_bytes = (
            (slots + 8) * long * LANES * 4
            + n_row * panels * many * long * block * 16
            + b_count * width * block * 8
            + panels * 2 * many * long * width * 4
        )
        made = pl.pallas_call(
            functools.partial(product_kernel, n_row, n_col, panels, sets, first, groups),
            out_shape=[jax.ShapeDtypeStruct(shape, jnp.float32) for shape in shapes],
            in_specs=[vmem] * (1 + n_row + n_col),
            out_specs=[vmem] * len(shapes),
            scratch_shapes=[
                pltpu.VMEM(((slots + 8) * long, LANES), jnp.float32),
                pltpu.VMEM((n_row * panels, 2 * many * long, 4 * block), jnp.bfloat16),
                pltpu.VMEM((b_count, 4 * block, width), jnp.bfloat16),
                pltpu.VMEM((panels, 2 * many * long, width), jnp.float32),
                pltpu.VMEM(((n_row + n_col * sets) * panels, LANES), jnp.float32),
                pltpu.VMEM((many * -(-n_row * panels * many // LANES), LANES), jnp.int32),
                pltpu.SMEM((many * -(-n_row * panels * many // LANES), LANES), jnp.int32),
                pltpu.SemaphoreType.DMA,
            ],
            compiler_params=room(held_bytes, scratch_bytes, slots * long * LANES * 4),
            cost_estimate=pl.CostEstimate(
                flops=n_row * panels * 2 * many * long * width * 4 * block * 2,
                bytes_accessed=held_bytes + slots * long * LANES * 4,
                transcendentals=0,
            ),
        )(table, *a_held, *b_held)
        return list(made[: len(groups)]), list(made[len(groups) :])

    order = far + near
    ((first, last),) = parts_of(pair)
    own, gone = products(first, last, [[m] for m in order], table)
    others, pieces = [], {}
    for at, m in enumerate(order):
        if at >= LAG_Y:
            gone[at], others[at - LAG_Y] = lax.optimization_barrier((gone[at], others[at - LAG_Y]))
        if at >= LAG_Z:
            key = order[at - LAG_Z], first
            gone[at], pieces[key] = lax.optimization_barrier((gone[at], pieces[key]))
        others.append(swap(gone[at], "layer", 1))
        total = own[at][0] + others[at][0]
        pieces[m, first] = swap(total, "row", m) if m else total
    keys = list(pieces)
    owned = pl.pallas_call(
        functools.partial(place_kernel, keys),
        out_shape=jax.ShapeDtypeStruct((n_row * CAP // 8, pair, 8, LANES), jnp.float32),
        in_specs=[vmem] * len(keys),
        out_specs=anywhere,
        scratch_shapes=[pltpu.SemaphoreType.DMA((len(keys),))],
        compiler_params=room(n_row * CAP * block * block * 4),
    )(*pieces.values())
    return owned.transpose(0, 2, 1, 3).reshape(n_row * CAP, block * block)


def solution(mesh):
    return jax.shard_map(
        body,
        mesh=mesh,
        in_specs=(
            P("col", "layer", "row", None, None, None),
            P("col", "layer", "row", None, None),
            P("row", "layer", "col", None, None, None, None),
            P("row", "layer", "col", None, None, None),
            P("col", "row", None),
            P("col", "row", None),
        ),
        out_specs=P(("layer", "row"), "col"),
        check_vma=False,
    )
```

```python
import functools
import jax
import jax.numpy as jnp
from jax import lax
from jax.experimental import pallas as pl
from jax.experimental.pallas import tpu as pltpu
from jax.sharding import PartitionSpec as P

TILE = 64
CAP = 16
LANES = 128
MIB = 2**20


def waits_of(at):
    return at - 4 if at >= 4 else None, 0 if at == 4 else at - 5 if at >= 6 else None


def swap(block, axis, mask):
    return lax.ppermute(block, axis, [(i, i ^ mask) for i in range(lax.axis_size(axis))])


def gathered(block, axis, order):
    held = {0: block}
    for mask in order:
        held[mask] = jax.tree.map(
            lambda x, low=mask & -mask: swap(x, axis, low), held[mask & (mask - 1)]
        )
    return [held[mask] for mask in range(lax.axis_size(axis))]


def gathered_with(block, axis, order, early):
    held = {0: block}
    for mask in order:
        source = held[mask & (mask - 1)]
        if mask == 3:
            source, early = lax.optimization_barrier((source, early))
            held[mask & (mask - 1)], done = source, early
        held[mask] = swap(source, axis, mask & -mask)
    return [held[mask] for mask in range(lax.axis_size(axis))], done


def parts_of(pair):
    return ((0, pair),)


def pack_a_kernel(a_ref, rows_ref, out_ref, flipped):
    panels, block, width = a_ref.shape
    half, pair, many = width // 2, block // 2, width // block
    for kk in range(panels):
        flipped[...] = a_ref[kk].T
        for first, last in parts_of(pair):
            long = last - first
            for a in range(many):
                at = kk * half + many * first + a * long
                for odd in range(2):
                    taken = flipped[pl.ds(a * block + 2 * first + odd, long, 2), :]
                    out_ref[pl.ds(at, long), odd * block : (odd + 1) * block] = taken
    out_ref[pl.ds(panels * half, 8), :] = jnp.zeros((8, LANES), jnp.float32)
    out_ref[pl.ds(panels * half, panels), :many] = rows_ref[...].astype(jnp.float32)


def pack_b_kernel(b_ref, cols_ref, out_ref):
    count, block, width = b_ref.shape

    @pl.loop(0, count)
    def _(i):
        out_ref[pl.ds(pl.multiple_of(i * block, block), block), :] = b_ref[i]

    out_ref[pl.ds(count * block, 8), :] = jnp.zeros((8, width), jnp.float32)
    out_ref[pl.ds(count * block, count), : cols_ref.shape[1]] = cols_ref[...].astype(jnp.float32)


def product_kernel(n_row, n_col, panels, sets, first, groups, table_ref, *refs):
    a_refs, refs = refs[:n_row], refs[n_row:]
    b_refs, refs = refs[:n_col], refs[n_col:]
    n_out = len(refs) - 8
    out_refs, refs = refs[:n_out], refs[n_out:]
    acc, left, right, prod, index, target, number, sem = refs
    block, width = right.shape[1] // 4, right.shape[2]
    many = width // block
    half = width // 2
    long = left.shape[1] // (2 * many)
    rows = many * long
    low = lax.broadcasted_iota(jnp.int32, (1, LANES), 1) < block

    my_row, my_col = lax.axis_index("row"), lax.axis_index("col")

    def place_b(m):
        label = lax.rem(lax.bitwise_xor(my_row, m) + my_col, n_row)
        offset = lax.rem(label - my_row + n_row, n_row)
        mask = lax.bitwise_xor(lax.rem(offset, n_col), my_col)
        return mask, lax.div(offset, n_col)

    count = n_row * panels
    for m in range(n_row):
        index[pl.ds(m * panels, panels), :] = a_refs[m][pl.ds(panels * half, panels), :]
    for m in range(n_col):
        tail = b_refs[m][pl.ds(sets * panels * block, sets * panels), pl.ds(0, LANES)]
        index[pl.ds(count + m * sets * panels, sets * panels), :] = tail
    down = index[pl.ds(0, count), :].T.astype(jnp.int32)
    across = lax.broadcasted_iota(jnp.int32, (many, LANES), 1)
    hot = [jnp.where(down[:many, k : k + 1] == across, 1.0, 0.0) for k in range(count)]
    hot = jnp.concatenate(hot, axis=0)[:, :TILE].astype(jnp.bfloat16)
    entries = table_ref[...]
    halves = [lax.shift_right_logical(entries, 4), lax.bitwise_and(entries, 15)]
    upper, lower = [
        jnp.dot(hot, x.astype(jnp.float32).astype(jnp.bfloat16), preferred_element_type=jnp.float32) for x in halves
    ]
    found = (upper * 16 + lower).astype(jnp.int32) * long
    per_row = LANES // many
    for k in range(count):
        mask, which = place_b(k // panels)
        at = count + (mask * sets + which) * panels + k % panels
        cols = jnp.broadcast_to(index[pl.ds(at, 1), :], (many, LANES)).astype(jnp.int32)
        picked = jnp.take_along_axis(found[k * many : (k + 1) * many, :], cols, axis=1)
        picked = jnp.where(across < many, picked, 0)
        shift = k % per_row * many
        picked = pltpu.roll(picked, shift, 1) if shift else picked
        group = pl.ds(k // per_row * many, many)
        target[group, :] = picked if shift == 0 else target[group, :] + picked
    copy = pltpu.make_async_copy(target, number, sem)
    copy.start()

    @pl.loop(0, acc.shape[0] // (8 * long))
    def _(i):
        acc[pl.ds(pl.multiple_of(i * 8 * long, 8), 8 * long), :] = jnp.zeros((8 * long, LANES), jnp.float32)

    for m in range(n_row):

        @pl.loop(0, panels, unroll=True)
        def _(kk, m=m):
            a = a_refs[m][pl.ds(pl.multiple_of(kk * half + many * first, 8), rows), :]
            turned = pltpu.roll(a, block, 1)
            rest = a - a.astype(jnp.bfloat16).astype(jnp.float32)
            turned_rest = pltpu.roll(rest, block, 1)
            at = m * panels + kk
            left[at, pl.ds(0, rows), pl.ds(0, LANES)] = jnp.where(low, a, turned).astype(jnp.bfloat16)
            left[at, pl.ds(0, rows), pl.ds(LANES, LANES)] = rest.astype(jnp.bfloat16)
            left[at, pl.ds(rows, rows), pl.ds(0, LANES)] = jnp.where(low, turned, a).astype(jnp.bfloat16)
            left[at, pl.ds(rows, rows), pl.ds(LANES, LANES)] = turned_rest.astype(jnp.bfloat16)

    for m in range(n_col):

        @pl.loop(0, sets * panels, unroll=True)
        def _(i, m=m):
            b = b_refs[m][pl.ds(pl.multiple_of(i * block, block), block), :]
            high = b.astype(jnp.bfloat16)
            rest = (b - high.astype(jnp.float32)).astype(jnp.bfloat16)
            at = m * sets * panels + i
            right[at, pl.ds(0, block), :] = high
            right[at, pl.ds(block, block), :] = rest
            right[at, pl.ds(2 * block, block), :] = high
            right[at, pl.ds(3 * block, block), :] = jnp.zeros_like(high)

    copy.wait()

    def multiply(m, kk):
        mask, which = place_b(m)
        prod[kk] = jnp.dot(
            left[m * panels + kk],
            right[(mask * sets + which) * panels + kk],
            preferred_element_type=jnp.float32,
        )

    def add(m, kk):
        k = m * panels + kk
        group, start = lax.div(k, per_row) * many, lax.rem(k, per_row) * many
        for a in range(many):
            places = [pl.multiple_of(number[group + a, start + b], 8) for b in range(many)]
            even = prod[kk, pl.ds(a * long, long), :]
            odd = prod[kk, pl.ds(rows + a * long, long), :]
            blocks = []
            for q in range(many // 2):
                e, o = even[:, q * LANES : (q + 1) * LANES], odd[:, q * LANES : (q + 1) * LANES]
                turned = pltpu.roll(jnp.where(low, o, e), block, 1)
                blocks += [jnp.where(low, e, turned), jnp.where(low, turned, o)]
            sums = [acc[pl.ds(at, long), :] + new for at, new in zip(places, blocks)]
            for at, new in zip(places, sums):
                acc[pl.ds(at, long), :] = new

    multiply(0, 0)

    @pl.loop(0, n_row, unroll=True)
    def _(m):
        for kk in range(panels):
            if kk + 1 < panels:
                multiply(m, kk + 1)
            else:
                multiply(lax.rem(m + 1, n_row), 0)
            add(m, kk)

    @pl.loop(0, long // 8)
    def _(j):
        at = pl.multiple_of(j * 8, 8)
        for out, out_ref in enumerate(out_refs):
            layer, group = divmod(out, len(groups))
            for i, m in enumerate(groups[group]):
                for eight in range(CAP // 8):
                    start = ((layer * n_row + m) * CAP + eight * 8) * long
                    taken = [acc[pl.ds(pl.multiple_of(start + s * long + at, 8), 8), :] for s in range(8)]
                    out_ref[i, eight, pl.ds(at, 8)] = jnp.swapaxes(jnp.stack(taken), 0, 1)


def place_kernel(pieces, *refs):
    sources, out_ref, sems = refs[: len(pieces)], refs[len(pieces)], refs[len(pieces) + 1]
    my_row = lax.axis_index("row")
    copies = []
    for i, (m, first) in enumerate(pieces):
        size, long = sources[i].shape[:2]
        at = pl.multiple_of(lax.bitwise_xor(my_row, m) * size, size)
        target = out_ref.at[pl.ds(at, size), pl.ds(first, long)]
        copies.append(pltpu.make_async_copy(sources[i], target, sems.at[i]))
    for copy in copies:
        copy.start()
    for copy in copies:
        copy.wait()


def body(a_val, a_rows, b_val, b_cols, pattern, owners):
    n_row, n_col, n_layer = (lax.axis_size(x) for x in ("row", "col", "layer"))
    panels, block, width = a_val.shape[3:]
    sets = b_val.shape[3]
    many = width // block
    pair = block // 2
    kept = pattern.shape[2]
    a_val, a_rows = a_val[0, 0, 0], a_rows[0, 0, 0]
    b_val = b_val[0, 0, 0].reshape(sets * panels, block, width)
    b_cols = b_cols[0, 0, 0].reshape(sets * panels, many)
    vmem, anywhere = pl.BlockSpec(memory_space=pltpu.VMEM), pl.BlockSpec(memory_space=pl.ANY)

    def room(*arrays):
        return pltpu.CompilerParams(vmem_limit_bytes=2 * MIB + sum(arrays))

    a_shape = (panels * width // 2 + 8, LANES)
    b_shape = (sets * panels * block + 8, width)

    a_packed = pl.pallas_call(
        pack_a_kernel,
        out_shape=jax.ShapeDtypeStruct(a_shape, jnp.float32),
        in_specs=[vmem] * 2,
        out_specs=vmem,
        scratch_shapes=[pltpu.VMEM((width, block), jnp.float32)],
        compiler_params=room(a_val.size * 8, width * LANES * 4),
    )(a_val, a_rows)
    b_packed = pl.pallas_call(
        pack_b_kernel,
        out_shape=jax.ShapeDtypeStruct(b_shape, jnp.float32),
        in_specs=[vmem] * 2,
        out_specs=vmem,
        compiler_params=room(b_val.size * 8),
    )(b_val, b_cols)
    b_held = gathered(b_packed, "col", range(1, n_col))

    owner = owners[0, :, 0]
    my_row, my_layer = lax.axis_index("row"), lax.axis_index("layer")
    before = (owner[:, None] == owner[None, :]) & (
        jnp.arange(kept)[None, :] < jnp.arange(kept)[:, None]
    )
    rank = jnp.sum(before.astype(jnp.int32), axis=1)
    unit = ((owner // n_row) ^ my_layer) * n_row + ((owner % n_row) ^ my_row)
    slots = n_layer * n_row * CAP
    slot = unit * CAP + rank
    codes = jnp.arange(TILE * TILE, dtype=jnp.int32)
    hit = codes[:, None] == pattern[0, 0][None, :]
    table = slots + jnp.sum(jnp.where(hit, slot[None, :] - slots, 0), axis=1)
    table = jnp.pad(table.reshape(TILE, TILE), ((0, 0), (0, LANES - TILE)))

    high_first = sorted(range(1, n_row), key=lambda m: (m & 1, m.bit_count(), -m))
    a_held, table = gathered_with(a_packed, "row", high_first, table)

    b_count = n_col * sets * panels
    held_bytes = n_row * a_shape[0] * LANES * 4 + n_col * b_shape[0] * width * 4
    far, near = list(range(n_row // 2, n_row)), [*range(2, n_row // 2), 1, 0]

    def products(first, last, groups, table):
        long = last - first
        shapes = [(len(g), CAP // 8, long, 8, LANES) for g in groups] * n_layer
        scratch_bytes = (
            (slots + 8) * long * LANES * 4
            + n_row * panels * many * long * block * 16
            + b_count * width * block * 8
            + panels * 2 * many * long * width * 4
        )
        made = pl.pallas_call(
            functools.partial(product_kernel, n_row, n_col, panels, sets, first, groups),
            out_shape=[jax.ShapeDtypeStruct(shape, jnp.float32) for shape in shapes],
            in_specs=[vmem] * (1 + n_row + n_col),
            out_specs=[vmem] * len(shapes),
            scratch_shapes=[
                pltpu.VMEM(((slots + 8) * long, LANES), jnp.float32),
                pltpu.VMEM((n_row * panels, 2 * many * long, 4 * block), jnp.bfloat16),
                pltpu.VMEM((b_count, 4 * block, width), jnp.bfloat16),
                pltpu.VMEM((panels, 2 * many * long, width), jnp.float32),
                pltpu.VMEM(((n_row + n_col * sets) * panels, LANES), jnp.float32),
                pltpu.VMEM((many * -(-n_row * panels * many // LANES), LANES), jnp.int32),
                pltpu.SMEM((many * -(-n_row * panels * many // LANES), LANES), jnp.int32),
                pltpu.SemaphoreType.DMA,
            ],
            compiler_params=room(held_bytes, scratch_bytes, slots * long * LANES * 4),
            cost_estimate=pl.CostEstimate(
                flops=n_row * panels * 2 * many * long * width * 4 * block * 2,
                bytes_accessed=held_bytes + slots * long * LANES * 4,
                transcendentals=0,
            ),
        )(table, *a_held, *b_held)
        return list(made[: len(groups)]), list(made[len(groups) :])

    order = far + near
    ((first, last),) = parts_of(pair)
    own, gone = products(first, last, [[m] for m in order], table)
    others, pieces = [], {}
    for at, m in enumerate(order):
        layer_done, row_done = waits_of(at)
        if layer_done is not None:
            gone[at], others[layer_done] = lax.optimization_barrier((gone[at], others[layer_done]))
        if row_done is not None:
            key = order[row_done], first
            gone[at], pieces[key] = lax.optimization_barrier((gone[at], pieces[key]))
        others.append(swap(gone[at], "layer", 1))
        total = own[at][0] + others[at][0]
        pieces[m, first] = swap(total, "row", m) if m else total
    keys = list(pieces)
    owned = pl.pallas_call(
        functools.partial(place_kernel, keys),
        out_shape=jax.ShapeDtypeStruct((n_row * CAP // 8, pair, 8, LANES), jnp.float32),
        in_specs=[vmem] * len(keys),
        out_specs=anywhere,
        scratch_shapes=[pltpu.SemaphoreType.DMA((len(keys),))],
        compiler_params=room(n_row * CAP * block * block * 4),
    )(*pieces.values())
    return owned.transpose(0, 2, 1, 3).reshape(n_row * CAP, block * block)


def solution(mesh):
    return jax.shard_map(
        body,
        mesh=mesh,
        in_specs=(
            P("col", "layer", "row", None, None, None),
            P("col", "layer", "row", None, None),
            P("row", "layer", "col", None, None, None, None),
            P("row", "layer", "col", None, None, None),
            P("col", "row", None),
            P("col", "row", None),
        ),
        out_specs=P(("layer", "row"), "col"),
        check_vma=False,
    )
```

```python
import functools
import jax
import jax.numpy as jnp
from jax import lax
from jax.experimental import pallas as pl
from jax.experimental.pallas import tpu as pltpu
from jax.sharding import PartitionSpec as P

TILE = 64
CAP = 16
LANES = 128
MIB = 2**20


def waits_of(at):
    return at - 4 if at >= 4 else None, 0 if at == 4 else at - 5 if at >= 6 else None


def swap(block, axis, mask):
    return lax.ppermute(block, axis, [(i, i ^ mask) for i in range(lax.axis_size(axis))])


def gathered(block, axis, order):
    held = {0: block}
    for mask in order:
        held[mask] = jax.tree.map(
            lambda x, low=mask & -mask: swap(x, axis, low), held[mask & (mask - 1)]
        )
    return [held[mask] for mask in range(lax.axis_size(axis))]


def gathered_with(block, axis, order, early):
    held = {0: block}
    for mask in order:
        source = held[mask & (mask - 1)]
        if mask == 3:
            source, early = lax.optimization_barrier((source, early))
            held[mask & (mask - 1)], done = source, early
        held[mask] = swap(source, axis, mask & -mask)
    return [held[mask] for mask in range(lax.axis_size(axis))], done


def parts_of(pair):
    return ((0, pair),)


def pack_a_kernel(a_ref, rows_ref, out_ref, flipped):
    panels, block, width = a_ref.shape
    half, pair, many = width // 2, block // 2, width // block
    for kk in range(panels):
        flipped[...] = a_ref[kk].T
        for first, last in parts_of(pair):
            long = last - first
            for a in range(many):
                at = kk * half + many * first + a * long
                for odd in range(2):
                    taken = flipped[pl.ds(a * block + 2 * first + odd, long, 2), :]
                    out_ref[pl.ds(at, long), odd * block : (odd + 1) * block] = taken
    out_ref[pl.ds(panels * half, 8), :] = jnp.zeros((8, LANES), jnp.float32)
    out_ref[pl.ds(panels * half, panels), :many] = rows_ref[...].astype(jnp.float32)


def pack_b_kernel(b_ref, cols_ref, out_ref):
    count, block, width = b_ref.shape

    @pl.loop(0, count)
    def _(i):
        out_ref[pl.ds(pl.multiple_of(i * block, block), block), :] = b_ref[i]

    out_ref[pl.ds(count * block, 8), :] = jnp.zeros((8, width), jnp.float32)
    out_ref[pl.ds(count * block, count), : cols_ref.shape[1]] = cols_ref[...].astype(jnp.float32)


def product_kernel(n_row, n_col, panels, sets, first, groups, table_ref, *refs):
    a_refs, refs = refs[:n_row], refs[n_row:]
    b_refs, refs = refs[:n_col], refs[n_col:]
    n_out = len(refs) - 8
    out_refs, refs = refs[:n_out], refs[n_out:]
    acc, left, right, prod, index, target, number, sem = refs
    block, width = right.shape[1] // 4, right.shape[2]
    many = width // block
    half = width // 2
    long = left.shape[1] // (2 * many)
    rows = many * long
    low = lax.broadcasted_iota(jnp.int32, (1, LANES), 1) < block

    my_row, my_col = lax.axis_index("row"), lax.axis_index("col")

    def place_b(m):
        label = lax.rem(lax.bitwise_xor(my_row, m) + my_col, n_row)
        offset = lax.rem(label - my_row + n_row, n_row)
        mask = lax.bitwise_xor(lax.rem(offset, n_col), my_col)
        return mask, lax.div(offset, n_col)

    count = n_row * panels
    for m in range(n_row):
        index[pl.ds(m * panels, panels), :] = a_refs[m][pl.ds(panels * half, panels), :]
    for m in range(n_col):
        tail = b_refs[m][pl.ds(sets * panels * block, sets * panels), pl.ds(0, LANES)]
        index[pl.ds(count + m * sets * panels, sets * panels), :] = tail
    down = index[pl.ds(0, count), :].T.astype(jnp.int32)
    across = lax.broadcasted_iota(jnp.int32, (many, LANES), 1)
    hot = [jnp.where(down[:many, k : k + 1] == across, 1.0, 0.0) for k in range(count)]
    hot = jnp.concatenate(hot, axis=0)[:, :TILE].astype(jnp.bfloat16)
    entries = table_ref[...]
    halves = [lax.shift_right_logical(entries, 4), lax.bitwise_and(entries, 15)]
    upper, lower = [
        jnp.dot(hot, x.astype(jnp.float32).astype(jnp.bfloat16), preferred_element_type=jnp.float32) for x in halves
    ]
    found = (upper * 16 + lower).astype(jnp.int32) * long
    per_row = LANES // many
    for k in range(count):
        mask, which = place_b(k // panels)
        at = count + (mask * sets + which) * panels + k % panels
        cols = jnp.broadcast_to(index[pl.ds(at, 1), :], (many, LANES)).astype(jnp.int32)
        picked = jnp.take_along_axis(found[k * many : (k + 1) * many, :], cols, axis=1)
        picked = jnp.where(across < many, picked, 0)
        shift = k % per_row * many
        picked = pltpu.roll(picked, shift, 1) if shift else picked
        group = pl.ds(k // per_row * many, many)
        target[group, :] = picked if shift == 0 else target[group, :] + picked
    copy = pltpu.make_async_copy(target, number, sem)
    copy.start()

    @pl.loop(0, acc.shape[0] // (8 * long))
    def _(i):
        acc[pl.ds(pl.multiple_of(i * 8 * long, 8), 8 * long), :] = jnp.zeros((8 * long, LANES), jnp.float32)

    for m in range(n_row):

        @pl.loop(0, panels, unroll=True)
        def _(kk, m=m):
            a = a_refs[m][pl.ds(pl.multiple_of(kk * half + many * first, 8), rows), :]
            turned = pltpu.roll(a, block, 1)
            rest = a - a.astype(jnp.bfloat16).astype(jnp.float32)
            turned_rest = pltpu.roll(rest, block, 1)
            at = m * panels + kk
            left[at, pl.ds(0, rows), pl.ds(0, LANES)] = jnp.where(low, a, turned).astype(jnp.bfloat16)
            left[at, pl.ds(0, rows), pl.ds(LANES, LANES)] = rest.astype(jnp.bfloat16)
            left[at, pl.ds(rows, rows), pl.ds(0, LANES)] = jnp.where(low, turned, a).astype(jnp.bfloat16)
            left[at, pl.ds(rows, rows), pl.ds(LANES, LANES)] = turned_rest.astype(jnp.bfloat16)

    for m in range(n_col):

        @pl.loop(0, sets * panels, unroll=True)
        def _(i, m=m):
            b = b_refs[m][pl.ds(pl.multiple_of(i * block, block), block), :]
            high = b.astype(jnp.bfloat16)
            rest = (b - high.astype(jnp.float32)).astype(jnp.bfloat16)
            at = m * sets * panels + i
            right[at, pl.ds(0, block), :] = high
            right[at, pl.ds(block, block), :] = rest
            right[at, pl.ds(2 * block, block), :] = high
            right[at, pl.ds(3 * block, block), :] = jnp.zeros_like(high)

    copy.wait()

    def multiply(m, kk):
        mask, which = place_b(m)
        prod[kk] = jnp.dot(
            left[m * panels + kk],
            right[(mask * sets + which) * panels + kk],
            preferred_element_type=jnp.float32,
        )

    def add(m, kk):
        k = m * panels + kk
        group, start = lax.div(k, per_row) * many, lax.rem(k, per_row) * many
        for a in range(many):
            places = [pl.multiple_of(number[group + a, start + b], 8) for b in range(many)]
            even = prod[kk, pl.ds(a * long, long), :]
            odd = prod[kk, pl.ds(rows + a * long, long), :]
            blocks = []
            for q in range(many // 2):
                e, o = even[:, q * LANES : (q + 1) * LANES], odd[:, q * LANES : (q + 1) * LANES]
                turned = pltpu.roll(jnp.where(low, o, e), block, 1)
                blocks += [jnp.where(low, e, turned), jnp.where(low, turned, o)]
            sums = [acc[pl.ds(at, long), :] + new for at, new in zip(places, blocks)]
            for at, new in zip(places, sums):
                acc[pl.ds(at, long), :] = new

    multiply(0, 0)

    @pl.loop(0, n_row, unroll=True)
    def _(m):
        for kk in range(panels):
            if kk + 1 < panels:
                multiply(m, kk + 1)
            else:
                multiply(lax.rem(m + 1, n_row), 0)
            add(m, kk)

    @pl.loop(0, long // 8)
    def _(j):
        at = pl.multiple_of(j * 8, 8)
        for out, out_ref in enumerate(out_refs):
            layer, group = divmod(out, len(groups))
            for i, m in enumerate(groups[group]):
                for eight in range(CAP // 8):
                    start = ((layer * n_row + m) * CAP + eight * 8) * long
                    taken = [acc[pl.ds(pl.multiple_of(start + s * long + at, 8), 8), :] for s in range(8)]
                    out_ref[i, eight, pl.ds(at, 8)] = jnp.swapaxes(jnp.stack(taken), 0, 1)


def place_kernel(masks, *refs):
    sources, out_ref, sems = refs[: len(masks)], refs[-2], refs[-1]
    my_row = lax.axis_index("row")
    copies = []
    for i, m in enumerate(masks):
        size = sources[i].shape[0]
        at = pl.multiple_of(lax.bitwise_xor(my_row, m) * size, size)
        copies.append(pltpu.make_async_copy(sources[i], out_ref.at[pl.ds(at, size)], sems.at[i]))
    for copy in copies:
        copy.start()
    for copy in copies:
        copy.wait()


def body(a_val, a_rows, b_val, b_cols, pattern, owners):
    n_row, n_col, n_layer = (lax.axis_size(x) for x in ("row", "col", "layer"))
    panels, block, width = a_val.shape[3:]
    sets = b_val.shape[3]
    many = width // block
    pair = block // 2
    kept = pattern.shape[2]
    a_val, a_rows = a_val[0, 0, 0], a_rows[0, 0, 0]
    b_val = b_val[0, 0, 0].reshape(sets * panels, block, width)
    b_cols = b_cols[0, 0, 0].reshape(sets * panels, many)
    vmem, anywhere = pl.BlockSpec(memory_space=pltpu.VMEM), pl.BlockSpec(memory_space=pl.ANY)

    def room(*arrays):
        return pltpu.CompilerParams(vmem_limit_bytes=2 * MIB + sum(arrays))

    a_shape = (panels * width // 2 + 8, LANES)
    b_shape = (sets * panels * block + 8, width)

    a_packed = pl.pallas_call(
        pack_a_kernel,
        out_shape=jax.ShapeDtypeStruct(a_shape, jnp.float32),
        in_specs=[vmem] * 2,
        out_specs=vmem,
        scratch_shapes=[pltpu.VMEM((width, block), jnp.float32)],
        compiler_params=room(a_val.size * 8, width * LANES * 4),
    )(a_val, a_rows)
    b_packed = pl.pallas_call(
        pack_b_kernel,
        out_shape=jax.ShapeDtypeStruct(b_shape, jnp.float32),
        in_specs=[vmem] * 2,
        out_specs=vmem,
        compiler_params=room(b_val.size * 8),
    )(b_val, b_cols)
    b_held = gathered(b_packed, "col", range(1, n_col))

    owner = owners[0, :, 0]
    my_row, my_layer = lax.axis_index("row"), lax.axis_index("layer")
    before = (owner[:, None] == owner[None, :]) & (
        jnp.arange(kept)[None, :] < jnp.arange(kept)[:, None]
    )
    rank = jnp.sum(before.astype(jnp.int32), axis=1)
    unit = ((owner // n_row) ^ my_layer) * n_row + ((owner % n_row) ^ my_row)
    slots = n_layer * n_row * CAP
    slot = unit * CAP + rank
    codes = jnp.arange(TILE * TILE, dtype=jnp.int32)
    hit = codes[:, None] == pattern[0, 0][None, :]
    table = slots + jnp.sum(jnp.where(hit, slot[None, :] - slots, 0), axis=1)
    table = jnp.pad(table.reshape(TILE, TILE), ((0, 0), (0, LANES - TILE)))

    high_first = sorted(range(1, n_row), key=lambda m: (m & 1, m.bit_count(), -m))
    a_held, table = gathered_with(a_packed, "row", high_first, table)

    b_count = n_col * sets * panels
    held_bytes = n_row * a_shape[0] * LANES * 4 + n_col * b_shape[0] * width * 4
    far, near = list(range(n_row // 2, n_row)), [*range(2, n_row // 2), 1, 0]

    def products(first, last, groups, table):
        long = last - first
        shapes = [(len(g), CAP // 8, long, 8, LANES) for g in groups] * n_layer
        scratch_bytes = (
            (slots + 8) * long * LANES * 4
            + n_row * panels * many * long * block * 16
            + b_count * width * block * 8
            + panels * 2 * many * long * width * 4
        )
        made = pl.pallas_call(
            functools.partial(product_kernel, n_row, n_col, panels, sets, first, groups),
            out_shape=[jax.ShapeDtypeStruct(shape, jnp.float32) for shape in shapes],
            in_specs=[vmem] * (1 + n_row + n_col),
            out_specs=[vmem] * len(shapes),
            scratch_shapes=[
                pltpu.VMEM(((slots + 8) * long, LANES), jnp.float32),
                pltpu.VMEM((n_row * panels, 2 * many * long, 4 * block), jnp.bfloat16),
                pltpu.VMEM((b_count, 4 * block, width), jnp.bfloat16),
                pltpu.VMEM((panels, 2 * many * long, width), jnp.float32),
                pltpu.VMEM(((n_row + n_col * sets) * panels, LANES), jnp.float32),
                pltpu.VMEM((many * -(-n_row * panels * many // LANES), LANES), jnp.int32),
                pltpu.SMEM((many * -(-n_row * panels * many // LANES), LANES), jnp.int32),
                pltpu.SemaphoreType.DMA,
            ],
            compiler_params=room(held_bytes, scratch_bytes, slots * long * LANES * 4),
            cost_estimate=pl.CostEstimate(
                flops=n_row * panels * 2 * many * long * width * 4 * block * 2,
                bytes_accessed=held_bytes + slots * long * LANES * 4,
                transcendentals=0,
            ),
        )(table, *a_held, *b_held)
        return list(made[: len(groups)]), list(made[len(groups) :])

    order = far[:-1] + near[:1] + far[-1:] + near[1:]
    ((first, last),) = parts_of(pair)
    own, gone = products(first, last, [[m] for m in order], table)
    others, pieces = [], {}
    for at, m in enumerate(order):
        layer_done, row_done = waits_of(at)
        if layer_done is not None:
            gone[at], others[layer_done] = lax.optimization_barrier((gone[at], others[layer_done]))
        if row_done is not None:
            key = order[row_done], first
            gone[at], pieces[key] = lax.optimization_barrier((gone[at], pieces[key]))
        others.append(swap(gone[at], "layer", 1))
        total = (own[at] + others[at]).reshape(own[at].shape[1:])
        pieces[m, first] = swap(total, "row", m) if m else total
    owned = []
    for masks in (order[: n_row // 2] + [0], order[n_row // 2 : -1]):
        placed = pl.pallas_call(
            functools.partial(place_kernel, masks),
            out_shape=jax.ShapeDtypeStruct((n_row * CAP // 8, pair, 8, LANES), jnp.float32),
            in_specs=[vmem] * len(masks) + [anywhere] * len(owned),
            out_specs=anywhere,
            input_output_aliases={len(masks): 0} if owned else {},
            scratch_shapes=[pltpu.SemaphoreType.DMA((len(masks),))],
            compiler_params=room(len(masks) * CAP * block * block * 4),
        )(*[pieces[m, first] for m in masks], *owned)
        owned = [placed]
    (owned,) = owned
    return owned.transpose(0, 2, 1, 3).reshape(n_row * CAP, block * block)


def solution(mesh):
    return jax.shard_map(
        body,
        mesh=mesh,
        in_specs=(
            P("col", "layer", "row", None, None, None),
            P("col", "layer", "row", None, None),
            P("row", "layer", "col", None, None, None, None),
            P("row", "layer", "col", None, None, None),
            P("col", "row", None),
            P("col", "row", None),
        ),
        out_specs=P(("layer", "row"), "col"),
        check_vma=False,
    )
```
